32 devices in a mesh: dom: 8 (over z, y), tile: 4 (over x, core).
Axes of the slice: x: 2, y: 2, z: 4, core: 2. Of those that a mesh axis runs over, the one named last changes fastest.
Arguments:
- embeddings: float32 [2048, 256], P(('dom', 'tile')), may hold values from -1.5 to 1.5
- adagrad_state: float32 [2048], P(('dom', 'tile')), may hold values from 0.1 to 2
- offsets: int32 [2], replicated, may hold values from 1 to 7, as said below
- lhs_rows: int32 [8, 2, 96, 128], P('dom', None, 'tile'), may hold values from 0 to 255
- rhs_rows: int32 [8, 2, 96, 128], P('dom', None, 'tile'), may hold values from 0 to 255
- neg_blocks: int32 [8, 2, 96], P('dom', None, 'tile'), may hold values from 0 to 1
- tile_counts: int32 [8, 2], P('dom'), may hold values from 12 to 72, as said below
Outputs:
- new_embeddings: float32 [2048, 256], P(('dom', 'tile'))
- new_state: float32 [2048], P(('dom', 'tile'))
The draws below stay inside these ranges and needn't reach their ends.
Inputs may be any that keep to these rules, and one draw needn't show every extreme that they name: `offsets`: in one round of every draw the offset has all bits of a partition number set. `tile_counts`: in every round some bucket has exactly 72 live tiles.
All inputs are finite; a program needn't handle non-finite values.
Results may differ from the reference program's by a relative error of at most 0.007.
Values may be sent and summed in bfloat16 or wider, within the bound.
A program may use at most 64 MiB of HBM per device.

```python
import math
import jax
import jax.numpy as jnp
from jax import lax

D = 256
TE = 128
ROWS = 256
SLOTS = 24
ROUNDS = 2
SLOTS_ALL = 96
NODES = 2048
N_DOM = 8
N_TILE = 4


def draw_offsets(key, part):
    first_key, second_key = jax.random.split(jax.random.fold_in(key, 11))
    picks = jax.random.randint(first_key, (ROUNDS,), 1, N_DOM, dtype=jnp.int32)
    chosen = jax.random.randint(second_key, (), 0, ROUNDS, dtype=jnp.int32)
    return jnp.where(jnp.arange(ROUNDS, dtype=jnp.int32) == chosen, N_DOM - 1, picks).astype(jnp.int32)


def draw_tile_counts(key, part):
    first_key, second_key = jax.random.split(jax.random.fold_in(key, 23))
    top = 3 * SLOTS * N_TILE // 4
    counts = jax.random.randint(first_key, (N_DOM, ROUNDS), SLOTS * N_TILE // 8, top + 1, dtype=jnp.int32)
    fullest = jax.random.randint(second_key, (ROUNDS,), 0, N_DOM, dtype=jnp.int32)
    hit = jnp.arange(N_DOM, dtype=jnp.int32)[:, None] == fullest[None, :]
    return jnp.where(hit, top, counts).astype(jnp.int32)


def set_ends(entries, own_key, low, high):
    extent = entries.shape
    index_at = [jax.random.randint(jax.random.fold_in(own_key, axis), (), 0, extent[axis]) for axis in range(len(extent))]
    entries = entries.at[tuple(index_at)].set(low)
    longest = extent.index(max(extent))
    index_at[longest] = (index_at[longest] + 1) % extent[longest]
    return entries.at[tuple(index_at)].set(high)


def block_scale(key, dims, cuts, smallest, top_value):
    factor_of, own = 1.0, jax.random.fold_in(key, 6)
    for position, blocks in cuts:
        steps = jnp.exp(jax.random.uniform(jax.random.fold_in(own, position), (blocks,), jnp.float32, smallest / len(cuts), top_value / len(cuts)))
        factor_of = factor_of * jnp.repeat(steps, dims[position] // blocks).reshape([-1 if axis == position else 1 for axis in range(len(dims))])
    return factor_of


def scatter_about(stream_key, extent, width, bound, cuts=(), held_as=jnp.bfloat16):
    result = width * jax.random.normal(stream_key, extent, jnp.float32)
    if cuts:
        result = result * block_scale(stream_key, extent, cuts, -0.22, 0.18)
    return jnp.clip(result, -bound, bound).astype(held_as)


def setup_inputs(seed: int = 0) -> dict:
    keys = jax.random.split(jax.random.key(seed), 8)
    embeddings = scatter_about(keys[0], (NODES, D), 0.25, 1.5, ((0, 32),), jnp.float32)
    adagrad_state = jnp.clip(jnp.exp(math.log(2.0) - 2.9957323 * jax.random.uniform(keys[1], (NODES,), jnp.float32) ** block_scale(keys[1], (NODES,), ((0, 32),), -0.2, 0.2)), 0.1, 2.0)
    offsets = draw_offsets(jax.random.fold_in(keys[7], 71), 0)
    lhs_rows = set_ends(jax.random.randint(keys[3], (N_DOM, ROUNDS, SLOTS_ALL, TE), 0, ROWS), jax.random.fold_in(keys[3], 1), 0, ROWS - 1).astype(jnp.int32)
    rhs_rows = set_ends(jax.random.randint(keys[4], (N_DOM, ROUNDS, SLOTS_ALL, TE), 0, ROWS), jax.random.fold_in(keys[4], 1), 0, ROWS - 1).astype(jnp.int32)
    neg_blocks = set_ends(jax.random.randint(keys[5], (N_DOM, ROUNDS, SLOTS_ALL), 0, ROWS // TE), jax.random.fold_in(keys[5], 1), 0, (ROWS // TE) - 1).astype(jnp.int32)
    tile_counts = draw_tile_counts(jax.random.fold_in(keys[7], 71), 0)
    return {"embeddings": embeddings, "adagrad_state": adagrad_state, "offsets": offsets, "lhs_rows": lhs_rows, "rhs_rows": rhs_rows, "neg_blocks": neg_blocks, "tile_counts": tile_counts}


LEARN_RATE = 0.5

def bucket(item):
    own, other, lhs, rhs, neg, count = item
    slots_all = lhs.shape[0]
    edges = lhs.shape[1]
    spread = jnp.arange(edges, dtype=jnp.int32)
    targets = jnp.concatenate([rhs, neg[:, None] * edges + spread[None, :]], axis=1).astype(jnp.int32)
    left = own[lhs].astype(jnp.float32)
    right = other[targets].astype(jnp.float32)
    scores = jnp.einsum('gid,gjd->gij', left, right, precision=lax.Precision.HIGHEST)
    positive = jnp.arange(2 * edges, dtype=jnp.int32)[None, :] == spread[:, None]
    coef = jnp.where(positive[None], -jax.nn.sigmoid(-scores), jax.nn.sigmoid(scores) / (2 * edges - 1))
    active = jnp.arange(slots_all, dtype=jnp.int32) < count
    coef = jnp.where(active[:, None, None], coef, jnp.float32(0.0)).astype(jnp.bfloat16)
    coef = lax.optimization_barrier(coef).astype(jnp.float32)
    grad_left = jnp.einsum('gij,gjd->gid', coef, right, precision=lax.Precision.HIGHEST)
    grad_right = jnp.einsum('gij,gid->gjd', coef, left, precision=lax.Precision.HIGHEST)
    blank = jnp.zeros((own.shape[0], own.shape[1]), jnp.float32)
    own_grad = blank.at[lhs.reshape(-1)].add(grad_left.reshape(-1, own.shape[1]))
    partner_grad = blank.at[targets.reshape(-1)].add(grad_right.reshape(-1, own.shape[1]))
    return (own_grad, partner_grad)

def reference(embeddings, adagrad_state, offsets, lhs_rows, rhs_rows, neg_blocks, tile_counts):
    table = embeddings.reshape(N_DOM, ROWS, D)
    state = adagrad_state.reshape(N_DOM, ROWS)
    parts = jnp.arange(N_DOM, dtype=jnp.int32)
    for rnd in range(ROUNDS):
        partner = jnp.bitwise_xor(parts, offsets[rnd]).astype(jnp.int32)
        low = table.astype(jnp.bfloat16)
        own_grad, partner_grad = lax.map(bucket, (low, low[partner], lhs_rows[:, rnd], rhs_rows[:, rnd], neg_blocks[:, rnd], tile_counts[:, rnd]))
        total = own_grad + partner_grad[partner]
        state = state + lax.optimization_barrier(jnp.mean(total * total, axis=2))
        table = table - LEARN_RATE * total / jnp.sqrt(state)[:, :, None]
    return (table.reshape(N_DOM * ROWS, D), state.reshape(N_DOM * ROWS))
```

```python
import functools

import jax
import jax.numpy as jnp
from jax import lax
from jax.experimental import pallas as pl
from jax.experimental.pallas import tpu as pltpu
from jax.sharding import PartitionSpec as P

ROUNDS = 2
LEARN_RATE = 0.5
MESH = pl.DeviceIdType.MESH
NEG_AT = 24
RHS_AT = 32
MSG = 64
LANES = 128
CHUNK = 8
BF = jnp.bfloat16
F32 = jnp.float32


def nt(a, b):
    return lax.dot_general(a, b, (((1,), (1,)), ((), ())), preferred_element_type=F32)


def tn(a, b):
    return lax.dot_general(a, b, (((0,), (0,)), ((), ())), preferred_element_type=F32)


class Item:
    def __init__(self, refs, fixed, offset, place):
        self.cur, self.recv, self.got, self.ssem, self.rsem, self.gs, self.gr = refs
        self.fixed, self.offset = fixed, offset
        self.dom, self.tile, self.n_dom, self.n_tile = place
        self.stages = 1 if fixed else self.n_dom.bit_length() - 1
        self.at = 0
        self.sends = []

    def start(self):
        if self.fixed:
            to = self.n_dom - 1 - self.dom
        else:
            to = flip_bit(self.dom, self.at)
        self.copy = pltpu.make_async_remote_copy(
            src_ref=self.cur.at[self.at],
            dst_ref=self.recv.at[self.at],
            send_sem=self.ssem.at[self.at],
            recv_sem=self.rsem.at[self.at],
            device_id=(to, self.tile),
            device_id_type=MESH,
        )
        self.copy.start()
        self.sends.append(self.copy)

    def advance(self):
        self.copy.wait_recv()
        if self.fixed:
            final = self.recv.at[0]
        else:
            new = self.recv[self.at].astype(F32)
            old = self.cur[self.at].astype(F32)
            bit = (self.offset >> self.at) & 1
            take = jnp.broadcast_to(bit, new.shape) == 1
            self.cur[self.at + 1] = jnp.where(take, new, old).astype(BF)
            final = self.cur.at[self.at + 1]
        self.at += 1
        if self.at < self.stages:
            self.start()
            return
        self.copies = spread(final, self.got, self.gs, self.gr, self.tile, self.dom, self.n_tile)
        self.sends += self.copies
        self.got[self.tile] = final[...]

    def finish(self):
        while self.at < self.stages:
            self.advance()

    def arrive(self):
        for copy in self.copies:
            copy.wait_recv()


def flip_bit(value, bit):
    step = 1 << bit
    return value + step - 2 * step * lax.rem(lax.div(value, step), 2)


def spread(src, got, send_sems, recv_sems, tile, dom, n_tile):
    copies = []
    for d in range(1, n_tile):
        copy = pltpu.make_async_remote_copy(
            src_ref=src,
            dst_ref=got.at[tile],
            send_sem=send_sems.at[d - 1],
            recv_sem=recv_sems.at[d - 1],
            device_id=(dom, lax.rem(tile + d, n_tile)),
            device_id_type=MESH,
        )
        copy.start()
        copies.append(copy)
    return copies


def kernel(direct0, n_dom, n_tile, senders, edges, *refs):
    offs, counts, neg, emb, state, lhs, rhs, out, out_state = refs[:9]
    items = [refs[9 + 7 * i : 16 + 7 * i] for i in range(4)]
    own_got, own_gs, own_gr, group, acc, own_cur = refs[37:]
    dom, tile = lax.axis_index("dom"), lax.axis_index("tile")
    quarter, width = emb.shape
    rows_all = quarter * n_tile
    slots = lhs.shape[1]
    bits = n_dom.bit_length() - 1

    barrier = pltpu.get_barrier_semaphore()
    peers = [(dom, lax.rem(tile + d, n_tile)) for d in range(1, n_tile)]
    peers += [(flip_bit(dom, bit), tile) for bit in range(bits)]
    peers += [(n_dom - 1 - dom, tile)]
    for peer in peers:
        pl.semaphore_signal(barrier, inc=1, device_id=peer, device_id_type=MESH)

    place = (dom, tile, n_dom, n_tile)
    table0 = Item(items[0], direct0, offs[0], place)
    rows0 = Item(items[1], direct0, offs[0], place)
    rows1 = Item(items[2], not direct0, offs[1], place)
    table1 = Item(items[3], not direct0, offs[1], place)

    lane = lax.broadcasted_iota(jnp.int32, (1, LANES), 1)
    slot_of = lax.broadcasted_iota(jnp.int32, (slots, edges), 0) + tile * slots
    low = emb[...].astype(BF)
    table0.cur[0] = low
    for rnd in range(ROUNDS):
        alive = slot_of < jnp.broadcast_to(counts[rnd], slot_of.shape)
        left = jnp.where(alive, lhs[rnd].astype(F32), -1.0)
        right = jnp.where(alive, rhs[rnd].astype(F32), -1.0)
        blocks = jnp.zeros((1, LANES), F32)
        for g in range(slots):
            value = jnp.broadcast_to(neg[rnd, g], blocks.shape).astype(F32)
            blocks = jnp.where(lane == tile * slots + g, value, blocks)
        pad = jnp.zeros((RHS_AT - slots, LANES), F32)
        first = lax.broadcasted_iota(jnp.int32, pad.shape, 0) == NEG_AT - slots
        packed = jnp.concatenate([left, jnp.where(first, blocks, 0.0), right, pad], axis=0)
        packed = packed.astype(BF)
        own_cur[rnd] = packed
        own_got[rnd, tile] = packed
        (rows0 if rnd == 0 else rows1).cur[0] = packed

    pl.semaphore_wait(barrier, len(peers))

    table0.start()
    rows0.start()
    own = [
        spread(own_cur.at[rnd], own_got.at[rnd], own_gs.at[rnd], own_gr.at[rnd], tile, dom, n_tile)
        for rnd in range(ROUNDS)
    ]
    rows1.start()

    chunks = slots // CHUNK
    span = CHUNK * edges
    slot_row = lax.broadcasted_iota(jnp.int32, (LANES, span), 0)
    edge_slot = lax.broadcasted_iota(jnp.int32, (LANES, span), 1) // edges

    def fill(i, carry):
        group[i] = jnp.where(slot_row == edge_slot + i * CHUNK, 1.0, 0.0).astype(BF)
        return carry

    lax.fori_loop(0, senders * chunks, fill, 0)

    key = lax.broadcasted_iota(jnp.int32, (rows_all, edges), 0).astype(F32)
    mine = (lax.broadcasted_iota(jnp.int32, (quarter, edges), 0) + tile * quarter).astype(F32)

    def count(which, got, swap):
        acc[which] = jnp.zeros(acc.shape[1:], F32)

        def body(s, carry):
            held = got[s].astype(F32)
            for chunk in range(chunks):
                keys, mines = [], []
                for g in range(chunk * CHUNK, (chunk + 1) * CHUNK):
                    src = held[g : g + 1]
                    dst = held[RHS_AT + g : RHS_AT + g + 1]
                    for_mine, for_key = (dst, src) if swap else (src, dst)
                    keys.append(jnp.where(key == for_key, 1.0, 0.0).astype(BF))
                    mines.append(jnp.where(mine == for_mine, 1.0, 0.0).astype(BF))
                pick_mine = jnp.concatenate(mines, axis=1)
                pick = jnp.concatenate([jnp.concatenate(keys, axis=1), pick_mine], axis=0)
                against = jnp.concatenate([group[s * chunks + chunk], pick_mine], axis=0)
                acc[which] += nt(pick, against)
            return carry

        lax.fori_loop(0, senders, body, 0)

    def neg_row(got):
        total = got[0, RHS_AT - 16 : RHS_AT].astype(F32)
        for s in range(1, senders):
            total = total + got[s, RHS_AT - 16 : RHS_AT].astype(F32)
        at = NEG_AT - RHS_AT + 16
        return total[at : at + 1]

    key_block = (lax.broadcasted_iota(jnp.int32, (rows_all, LANES), 0) // edges).astype(F32)
    mine_block = (
        (lax.broadcasted_iota(jnp.int32, (quarter, LANES), 0) + tile * quarter) // edges
    ).astype(F32)

    def pair_counts(rnd, own_rows, other_rows):
        a, b = 2 * rnd, 2 * rnd + 1
        own_key = acc[a, :rows_all, :LANES] + jnp.where(key_block == neg_row(own_rows), 1.0, 0.0)
        own_mine = acc[a, rows_all:, :LANES]
        other_key = acc[b, :rows_all, :LANES]
        other_mine = acc[b, rows_all:, :LANES] + jnp.where(
            mine_block == neg_row(other_rows), 1.0, 0.0
        )
        every = nt(
            jnp.concatenate([own_key, other_key], axis=1).astype(BF),
            jnp.concatenate([own_mine, other_mine], axis=1).astype(BF),
        )
        positive = acc[a, :rows_all, LANES:] + acc[b, :rows_all, LANES:]
        return every - positive, positive

    eye = lax.broadcasted_iota(jnp.int32, (quarter, quarter), 0) == lax.broadcasted_iota(
        jnp.int32, (quarter, quarter), 1
    )

    def update(low, got, pairs, table, held):
        negative, positive = pairs
        other = jnp.concatenate([got[s] for s in range(n_tile)], axis=0)
        scores = nt(other, low)
        off_coef = (jax.nn.sigmoid(scores) / (2 * edges - 1)).astype(BF).astype(F32)
        on_coef = (-jax.nn.sigmoid(-scores)).astype(BF).astype(F32)
        weight = negative * off_coef + positive * on_coef
        high = weight.astype(BF)
        rest = (weight - high.astype(F32)).astype(BF)
        both = tn(jnp.concatenate([high, rest], axis=1), other)
        total = both[:quarter] + both[quarter:]
        held = held + jnp.sum(total * total, axis=1, keepdims=True) / width
        return table - LEARN_RATE * total / jnp.sqrt(held), held

    for copy in own[0]:
        copy.wait_recv()
    count(0, own_got.at[0], False)
    while table0.at < table0.stages:
        table0.advance()
        rows0.advance()
    rows1.advance()
    for copy in own[1]:
        copy.wait_recv()
    count(2, own_got.at[1], False)
    rows1.finish()
    rows0.arrive()
    count(1, rows0.got, True)
    pairs = pair_counts(0, own_got.at[0], rows0.got)
    table0.arrive()
    held = jnp.sum(jnp.where(eye, state[...], 0.0), axis=1, keepdims=True)
    table, held = update(low, table0.got, pairs, emb[...], held)
    low = table.astype(BF)
    table1.cur[0] = low
    out[...] = table
    table1.start()
    rows1.arrive()
    count(3, rows1.got, True)
    pairs = pair_counts(1, own_got.at[1], rows1.got)
    table1.finish()
    table1.arrive()
    table, held = update(table1.cur[0], table1.got, pairs, out[...], held)
    out[...] = table
    out_state[...] = jnp.sum(jnp.where(eye, held, 0.0), axis=0, keepdims=True)
    for copy in table0.sends + rows0.sends + rows1.sends + table1.sends + own[0] + own[1]:
        copy.wait_send()


def shards(n_dom, n_tile, embeddings, adagrad_state, offsets, lhs_rows, rhs_rows, neg_blocks, tile_counts):
    quarter, width = embeddings.shape
    slots, edges = lhs_rows.shape[2], lhs_rows.shape[3]
    rows_all = quarter * n_tile
    bits = n_dom.bit_length() - 1
    senders = (3 * n_tile + 3) // 4
    dma = pltpu.SemaphoreType.DMA

    def item(rows, lanes):
        return [
            pltpu.VMEM((bits + 1, rows, lanes), BF),
            pltpu.VMEM((bits, rows, lanes), BF),
            pltpu.VMEM((n_tile, rows, lanes), BF),
            dma((bits,)),
            dma((bits,)),
            dma((n_tile - 1,)),
            dma((n_tile - 1,)),
        ]

    smem = pl.BlockSpec(memory_space=pltpu.SMEM)
    vmem = pl.BlockSpec(memory_space=pltpu.VMEM)

    def call(direct0, *args):
        return pl.pallas_call(
            functools.partial(kernel, direct0, n_dom, n_tile, senders, edges),
            out_shape=(
                jax.ShapeDtypeStruct((quarter, width), F32),
                jax.ShapeDtypeStruct((1, quarter), F32),
            ),
            in_specs=[smem] * 3 + [vmem] * 4,
            out_specs=(vmem, vmem),
            scratch_shapes=item(quarter, width)
            + item(MSG, LANES)
            + item(MSG, LANES)
            + item(quarter, width)
            + [
                pltpu.VMEM((ROUNDS, n_tile, MSG, LANES), BF),
                dma((ROUNDS, n_tile - 1)),
                dma((ROUNDS, n_tile - 1)),
                pltpu.VMEM((senders * slots // CHUNK, LANES, CHUNK * edges), BF),
                pltpu.VMEM((2 * ROUNDS, rows_all + quarter, LANES + quarter), F32),
                pltpu.VMEM((ROUNDS, MSG, LANES), BF),
            ],
            compiler_params=pltpu.CompilerParams(
                collective_id=0 if direct0 else 1,
                has_side_effects=True,
                vmem_limit_bytes=40 << 20,
            ),
        )(*args)

    table, state = lax.cond(
        offsets[0] == n_dom - 1,
        functools.partial(call, True),
        functools.partial(call, False),
        offsets,
        tile_counts[0],
        neg_blocks[0],
        embeddings,
        adagrad_state.reshape(1, quarter),
        lhs_rows[0],
        rhs_rows[0],
    )
    return table, state.reshape(quarter)


def solution(mesh):
    return jax.shard_map(
        functools.partial(shards, mesh.shape["dom"], mesh.shape["tile"]),
        mesh=mesh,
        in_specs=(
            P(("dom", "tile"), None),
            P(("dom", "tile")),
            P(),
            P("dom", None, "tile", None),
            P("dom", None, "tile", None),
            P("dom", None, "tile"),
            P("dom", None),
        ),
        out_specs=(P(("dom", "tile"), None), P(("dom", "tile"))),
        check_vma=False,
    )
```

```python
import functools

import jax
import jax.numpy as jnp
from jax import lax
from jax.experimental import pallas as pl
from jax.experimental.pallas import tpu as pltpu
from jax.sharding import PartitionSpec as P

ROUNDS = 2
LEARN_RATE = 0.5
MESH = pl.DeviceIdType.MESH
NEG_AT = 24
RHS_AT = 32
MSG = 64
LANES = 128
DIRECT_MAX = 8
CHUNK = 8
BF = jnp.bfloat16
F32 = jnp.float32


def nt(a, b):
    return lax.dot_general(a, b, (((1,), (1,)), ((), ())), preferred_element_type=F32)


def tn(a, b):
    return lax.dot_general(a, b, (((0,), (0,)), ((), ())), preferred_element_type=F32)


class Item:
    def __init__(self, refs, mask, offset, place):
        self.cur, self.recv, self.got, self.ssem, self.rsem, self.gs, self.gr = refs
        self.mask, self.offset = mask, offset
        self.fixed = mask is not None
        self.dom, self.tile, self.n_dom, self.n_tile = place
        self.stages = 1 if self.fixed else self.n_dom.bit_length() - 1
        self.at = 0
        self.sends = []

    def start(self):
        if self.fixed:
            to = flip_bits(self.dom, self.mask)
        else:
            to = flip_bit(self.dom, self.at)
        self.copy = pltpu.make_async_remote_copy(
            src_ref=self.cur.at[self.at],
            dst_ref=self.recv.at[self.at],
            send_sem=self.ssem.at[self.at],
            recv_sem=self.rsem.at[self.at],
            device_id=(to, self.tile),
            device_id_type=MESH,
        )
        self.copy.start()
        self.sends.append(self.copy)

    def advance(self):
        self.copy.wait_recv()
        if self.fixed:
            final = self.recv.at[0]
        else:
            new = self.recv[self.at].astype(F32)
            old = self.cur[self.at].astype(F32)
            bit = (self.offset >> self.at) & 1
            take = jnp.broadcast_to(bit, new.shape) == 1
            self.cur[self.at + 1] = jnp.where(take, new, old).astype(BF)
            final = self.cur.at[self.at + 1]
        self.at += 1
        if self.at < self.stages:
            self.start()
            return
        self.copies = spread(final, self.got, self.gs, self.gr, self.tile, self.dom, self.n_tile)
        self.sends += self.copies
        self.got[self.tile] = final[...]

    def finish(self):
        while self.at < self.stages:
            self.advance()

    def arrive(self):
        for copy in self.copies:
            copy.wait_recv()


def flip_bit(value, bit):
    step = 1 << bit
    return value + step - 2 * step * lax.rem(lax.div(value, step), 2)


def flip_bits(value, mask):
    other = value
    for bit in range(mask.bit_length()):
        if mask >> bit & 1:
            other = flip_bit(other, bit)
    return other


def spread(src, got, send_sems, recv_sems, tile, dom, n_tile):
    copies = []
    for d in range(1, n_tile):
        copy = pltpu.make_async_remote_copy(
            src_ref=src,
            dst_ref=got.at[tile],
            send_sem=send_sems.at[d - 1],
            recv_sem=recv_sems.at[d - 1],
            device_id=(dom, lax.rem(tile + d, n_tile)),
            device_id_type=MESH,
        )
        copy.start()
        copies.append(copy)
    return copies


def kernel(mask0, mask1, n_dom, n_tile, senders, edges, *refs):
    offs, counts, neg, emb, state, lhs, rhs, out, out_state = refs[:9]
    items = [refs[9 + 7 * i : 16 + 7 * i] for i in range(4)]
    own_got, own_gs, own_gr, group, acc, own_cur = refs[37:]
    dom, tile = lax.axis_index("dom"), lax.axis_index("tile")
    quarter, width = emb.shape
    rows_all = quarter * n_tile
    slots = lhs.shape[1]
    bits = n_dom.bit_length() - 1

    barrier = pltpu.get_barrier_semaphore()
    peers = [(dom, lax.rem(tile + d, n_tile)) for d in range(1, n_tile)]
    if mask0 is None or mask1 is None:
        peers += [(flip_bit(dom, bit), tile) for bit in range(bits)]
    peers += [(flip_bits(dom, mask), tile) for mask in sorted({mask0, mask1} - {None})]
    for peer in peers:
        pl.semaphore_signal(barrier, inc=1, device_id=peer, device_id_type=MESH)

    place = (dom, tile, n_dom, n_tile)
    table0 = Item(items[0], mask0, offs[0], place)
    rows0 = Item(items[1], mask0, offs[0], place)
    rows1 = Item(items[2], mask1, offs[1], place)
    table1 = Item(items[3], mask1, offs[1], place)

    lane = lax.broadcasted_iota(jnp.int32, (1, LANES), 1)
    slot_of = lax.broadcasted_iota(jnp.int32, (slots, edges), 0) + tile * slots
    low = emb[...].astype(BF)
    table0.cur[0] = low
    for rnd in range(ROUNDS):
        alive = slot_of < jnp.broadcast_to(counts[rnd], slot_of.shape)
        left = jnp.where(alive, lhs[rnd].astype(F32), -1.0)
        right = jnp.where(alive, rhs[rnd].astype(F32), -1.0)
        blocks = jnp.zeros((1, LANES), F32)
        for g in range(slots):
            value = jnp.broadcast_to(neg[rnd, g], blocks.shape).astype(F32)
            blocks = jnp.where(lane == tile * slots + g, value, blocks)
        pad = jnp.zeros((RHS_AT - slots, LANES), F32)
        first = lax.broadcasted_iota(jnp.int32, pad.shape, 0) == NEG_AT - slots
        packed = jnp.concatenate([left, jnp.where(first, blocks, 0.0), right, pad], axis=0)
        packed = packed.astype(BF)
        own_cur[rnd] = packed
        own_got[rnd, tile] = packed
        (rows0 if rnd == 0 else rows1).cur[0] = packed

    pl.semaphore_wait(barrier, len(peers))

    own = []
    rows0.start()
    for rnd in range(ROUNDS):
        own.append(
            spread(
                own_cur.at[rnd], own_got.at[rnd], own_gs.at[rnd], own_gr.at[rnd], tile, dom, n_tile
            )
        )
        (table0 if rnd == 0 else rows1).start()

    chunks = slots // CHUNK
    span = CHUNK * edges
    slot_row = lax.broadcasted_iota(jnp.int32, (LANES, span), 0)
    edge_slot = lax.broadcasted_iota(jnp.int32, (LANES, span), 1) // edges

    def fill(i, carry):
        group[i] = jnp.where(slot_row == edge_slot + i * CHUNK, 1.0, 0.0).astype(BF)
        return carry

    lax.fori_loop(0, senders * chunks, fill, 0)

    key = lax.broadcasted_iota(jnp.int32, (rows_all, edges), 0).astype(F32).astype(BF)
    mine = lax.broadcasted_iota(jnp.int32, (quarter, edges), 0) + tile * quarter
    mine = mine.astype(F32).astype(BF)
    one, zero = jnp.ones((), BF), jnp.zeros((), BF)

    def count(which, got, swap, first, last):
        if first == 0:
            acc[which] = jnp.zeros(acc.shape[1:], F32)

        def body(s, carry):
            held = got[s]
            for chunk in range(chunks):
                keys, mines = [], []
                for g in range(chunk * CHUNK, (chunk + 1) * CHUNK):
                    src = held[g : g + 1]
                    dst = held[RHS_AT + g : RHS_AT + g + 1]
                    for_mine, for_key = (dst, src) if swap else (src, dst)
                    keys.append(jnp.where(key == for_key, one, zero))
                    mines.append(jnp.where(mine == for_mine, one, zero))
                pick_mine = jnp.concatenate(mines, axis=1)
                pick = jnp.concatenate([jnp.concatenate(keys, axis=1), pick_mine], axis=0)
                against = jnp.concatenate([group[s * chunks + chunk], pick_mine], axis=0)
                acc[which] += nt(pick, against)
            return carry

        lax.fori_loop(first, last, body, 0)

    def neg_row(got):
        total = got[0, RHS_AT - 16 : RHS_AT].astype(F32)
        for s in range(1, senders):
            total = total + got[s, RHS_AT - 16 : RHS_AT].astype(F32)
        at = NEG_AT - RHS_AT + 16
        return total[at : at + 1]

    key_block = (lax.broadcasted_iota(jnp.int32, (rows_all, LANES), 0) // edges).astype(F32)
    mine_block = (
        (lax.broadcasted_iota(jnp.int32, (quarter, LANES), 0) + tile * quarter) // edges
    ).astype(F32)

    def pair_counts(rnd, own_rows, other_rows):
        a, b = 2 * rnd, 2 * rnd + 1
        own_key = acc[a, :rows_all, :LANES] + jnp.where(key_block == neg_row(own_rows), 1.0, 0.0)
        own_mine = acc[a, rows_all:, :LANES]
        other_key = acc[b, :rows_all, :LANES]
        other_mine = acc[b, rows_all:, :LANES] + jnp.where(
            mine_block == neg_row(other_rows), 1.0, 0.0
        )
        every = nt(
            jnp.concatenate([own_key, other_key], axis=1).astype(BF),
            jnp.concatenate([own_mine, other_mine], axis=1).astype(BF),
        )
        positive = acc[a, :rows_all, LANES:] + acc[b, :rows_all, LANES:]
        return every - positive, positive

    eye = lax.broadcasted_iota(jnp.int32, (quarter, quarter), 0) == lax.broadcasted_iota(
        jnp.int32, (quarter, quarter), 1
    )

    def update(low, got, pairs, table, held):
        negative, positive = pairs
        other = jnp.concatenate([got[s] for s in range(n_tile)], axis=0)
        scores = nt(other, low)
        off_coef = (jax.nn.sigmoid(scores) / (2 * edges - 1)).astype(BF).astype(F32)
        on_coef = (-jax.nn.sigmoid(-scores)).astype(BF).astype(F32)
        weight = negative * off_coef + positive * on_coef
        high = weight.astype(BF)
        rest = (weight - high.astype(F32)).astype(BF)
        both = tn(jnp.concatenate([high, rest], axis=1), other)
        total = both[:quarter] + both[quarter:]
        held = held + jnp.sum(total * total, axis=1, keepdims=True) / width
        return table - LEARN_RATE * total / jnp.sqrt(held), held

    most = max(senders - 1, 1)
    for copy in own[0]:
        copy.wait_recv()
    count(0, own_got.at[0], False, 0, senders)
    while table0.at < table0.stages:
        rows0.advance()
        table0.advance()
    rows1.finish()
    for copy in own[1]:
        copy.wait_recv()
    count(2, own_got.at[1], False, 0, most)
    rows0.arrive()
    count(1, rows0.got, True, 0, senders)
    pairs = pair_counts(0, own_got.at[0], rows0.got)
    table0.arrive()
    held = jnp.sum(jnp.where(eye, state[...], 0.0), axis=1, keepdims=True)
    table, held = update(low, table0.got, pairs, emb[...], held)
    low = table.astype(BF)
    table1.cur[0] = low
    out[...] = table
    table1.start()
    count(2, own_got.at[1], False, most, senders)
    rows1.arrive()
    count(3, rows1.got, True, 0, most)
    table1.finish()
    count(3, rows1.got, True, most, senders)
    pairs = pair_counts(1, own_got.at[1], rows1.got)
    table1.arrive()
    table, held = update(table1.cur[0], table1.got, pairs, out[...], held)
    out[...] = table
    out_state[...] = jnp.sum(jnp.where(eye, held, 0.0), axis=0, keepdims=True)
    for copy in table0.sends + rows0.sends + rows1.sends + table1.sends + own[0] + own[1]:
        copy.wait_send()


def shards(n_dom, n_tile, embeddings, adagrad_state, offsets, lhs_rows, rhs_rows, neg_blocks, tile_counts):
    quarter, width = embeddings.shape
    slots, edges = lhs_rows.shape[2], lhs_rows.shape[3]
    rows_all = quarter * n_tile
    bits = n_dom.bit_length() - 1
    senders = (3 * n_tile + 3) // 4
    dma = pltpu.SemaphoreType.DMA

    def item(rows, lanes):
        return [
            pltpu.VMEM((bits + 1, rows, lanes), BF),
            pltpu.VMEM((bits, rows, lanes), BF),
            pltpu.VMEM((n_tile, rows, lanes), BF),
            dma((bits,)),
            dma((bits,)),
            dma((n_tile - 1,)),
            dma((n_tile - 1,)),
        ]

    smem = pl.BlockSpec(memory_space=pltpu.SMEM)
    vmem = pl.BlockSpec(memory_space=pltpu.VMEM)

    def call(mask0, mask1, ident, *args):
        return pl.pallas_call(
            functools.partial(kernel, mask0, mask1, n_dom, n_tile, senders, edges),
            out_shape=(
                jax.ShapeDtypeStruct((quarter, width), F32),
                jax.ShapeDtypeStruct((1, quarter), F32),
            ),
            in_specs=[smem] * 3 + [vmem] * 4,
            out_specs=(vmem, vmem),
            scratch_shapes=item(quarter, width)
            + item(MSG, LANES)
            + item(MSG, LANES)
            + item(quarter, width)
            + [
                pltpu.VMEM((ROUNDS, n_tile, MSG, LANES), BF),
                dma((ROUNDS, n_tile - 1)),
                dma((ROUNDS, n_tile - 1)),
                pltpu.VMEM((senders * slots // CHUNK, LANES, CHUNK * edges), BF),
                pltpu.VMEM((2 * ROUNDS, rows_all + quarter, LANES + quarter), F32),
                pltpu.VMEM((ROUNDS, MSG, LANES), BF),
            ],
            compiler_params=pltpu.CompilerParams(
                collective_id=ident,
                has_side_effects=True,
                vmem_limit_bytes=40 << 20,
            ),
        )(*args)

    full = n_dom - 1
    if n_dom <= DIRECT_MAX:
        cases = [(full, mask) for mask in range(1, n_dom)]
        cases += [(mask, full) for mask in range(1, full)]
        case = jnp.where(offsets[0] == full, offsets[1] - 1, full + offsets[0] - 1)
    else:
        cases = [(full, None), (None, full)]
        case = jnp.where(offsets[0] == full, 0, 1)
    table, state = lax.switch(
        case,
        [functools.partial(call, *masks, ident) for ident, masks in enumerate(cases)],
        offsets,
        tile_counts[0],
        neg_blocks[0],
        embeddings,
        adagrad_state.reshape(1, quarter),
        lhs_rows[0],
        rhs_rows[0],
    )
    return table, state.reshape(quarter)


def solution(mesh):
    return jax.shard_map(
        functools.partial(shards, mesh.shape["dom"], mesh.shape["tile"]),
        mesh=mesh,
        in_specs=(
            P(("dom", "tile"), None),
            P(("dom", "tile")),
            P(),
            P("dom", None, "tile", None),
            P("dom", None, "tile", None),
            P("dom", None, "tile"),
            P("dom", None),
        ),
        out_specs=(P(("dom", "tile"), None), P(("dom", "tile"))),
        check_vma=False,
    )
```

```python
import functools

import jax
import jax.numpy as jnp
from jax import lax
from jax.experimental import pallas as pl
from jax.experimental.pallas import tpu as pltpu
from jax.sharding import PartitionSpec as P

ROUNDS = 2
LEARN_RATE = 0.5
MESH = pl.DeviceIdType.MESH
PACK = 16
LANES = 128
DIRECT_MAX = 2
CHUNK = 8
BF = jnp.bfloat16
F32 = jnp.float32


def nt(a, b):
    return lax.dot_general(a, b, (((1,), (1,)), ((), ())), preferred_element_type=F32)


def tn(a, b):
    return lax.dot_general(a, b, (((0,), (0,)), ((), ())), preferred_element_type=F32)


class Item:
    def __init__(self, refs, mask, offset, place):
        self.cur, self.recv, self.got, self.ssem, self.rsem, self.gs, self.gr = refs
        self.mask, self.offset = mask, offset
        self.fixed = mask is not None
        self.dom, self.tile, self.n_dom, self.n_tile = place
        self.stages = 1 if self.fixed else self.n_dom.bit_length() - 1
        self.at = 0
        self.sends = []

    def start(self):
        if self.fixed:
            to = flip_bits(self.dom, self.mask)
        else:
            to = flip_bit(self.dom, self.at)
        self.copy = pltpu.make_async_remote_copy(
            src_ref=self.cur.at[self.at],
            dst_ref=self.recv.at[self.at],
            send_sem=self.ssem.at[self.at],
            recv_sem=self.rsem.at[self.at],
            device_id=(to, self.tile),
            device_id_type=MESH,
        )
        self.copy.start()
        self.sends.append(self.copy)

    def advance(self):
        self.copy.wait_recv()
        if self.fixed:
            final = self.recv.at[0]
        else:
            new = self.recv[self.at].astype(F32)
            old = self.cur[self.at].astype(F32)
            bit = (self.offset >> self.at) & 1
            take = jnp.broadcast_to(bit, new.shape) == 1
            self.cur[self.at + 1] = jnp.where(take, new, old).astype(BF)
            final = self.cur.at[self.at + 1]
        self.at += 1
        if self.at < self.stages:
            self.start()
            return
        self.copies = spread(final, self.got, self.gs, self.gr, self.tile, self.dom, self.n_tile)
        self.sends += self.copies
        self.got[self.tile] = final[...]

    def finish(self):
        while self.at < self.stages:
            self.advance()

    def arrive(self):
        for copy in self.copies:
            copy.wait_recv()


def flip_bit(value, bit):
    step = 1 << bit
    return value + step - 2 * step * lax.rem(lax.div(value, step), 2)


def flip_bits(value, mask):
    other = value
    for bit in range(mask.bit_length()):
        if mask >> bit & 1:
            other = flip_bit(other, bit)
    return other


def spread(src, got, send_sems, recv_sems, tile, dom, n_tile):
    copies = []
    for d in range(1, n_tile):
        copy = pltpu.make_async_remote_copy(
            src_ref=src,
            dst_ref=got.at[tile],
            send_sem=send_sems.at[d - 1],
            recv_sem=recv_sems.at[d - 1],
            device_id=(dom, lax.rem(tile + d, n_tile)),
            device_id_type=MESH,
        )
        copy.start()
        copies.append(copy)
    return copies


def kernel(mask0, mask1, n_dom, n_tile, senders, edges, *refs):
    offs, counts, neg, emb, state, lhs, rhs, out, out_state = refs[:9]
    items = [refs[9 + 7 * i : 16 + 7 * i] for i in range(4)]
    own_got, own_gs, own_gr, group, acc, own_cur = refs[37:]
    dom, tile = lax.axis_index("dom"), lax.axis_index("tile")
    quarter, width = emb.shape
    rows_all = quarter * n_tile
    slots = lhs.shape[1]
    bits = n_dom.bit_length() - 1

    barrier = pltpu.get_barrier_semaphore()
    peers = [(dom, lax.rem(tile + d, n_tile)) for d in range(1, n_tile)]
    if mask0 is None or mask1 is None:
        peers += [(flip_bit(dom, bit), tile) for bit in range(bits)]
    peers += [(flip_bits(dom, mask), tile) for mask in sorted({mask0, mask1} - {None})]
    for peer in peers:
        pl.semaphore_signal(barrier, inc=1, device_id=peer, device_id_type=MESH)

    place = (dom, tile, n_dom, n_tile)
    table0 = Item(items[0], mask0, offs[0], place)
    rows0 = Item(items[1], mask0, offs[0], place)
    rows1 = Item(items[2], mask1, offs[1], place)
    table1 = Item(items[3], mask1, offs[1], place)

    lane = lax.broadcasted_iota(jnp.int32, (1, LANES), 1)
    slot_of = lax.broadcasted_iota(jnp.int32, (slots, edges), 0) + tile * slots
    low = emb[...].astype(BF)
    table0.cur[0] = low
    for rnd in range(ROUNDS):
        alive = slot_of < jnp.broadcast_to(counts[rnd], slot_of.shape)
        left = jnp.where(alive, lhs[rnd].astype(F32), -1.0)
        right = jnp.where(alive, rhs[rnd].astype(F32), -1.0)
        blocks = jnp.zeros((1, LANES), F32)
        for g in range(slots):
            value = jnp.broadcast_to(neg[rnd, g], blocks.shape).astype(F32)
            blocks = jnp.where(lane == tile * slots + g, value, blocks)
        parts = []
        for at in range(0, slots, CHUNK):
            parts += [left[at : at + CHUNK], right[at : at + CHUNK]]
        parts.append(jnp.broadcast_to(blocks, (PACK, LANES)))
        packed = jnp.concatenate(parts, axis=0).astype(BF)
        own_cur[rnd] = packed
        own_got[rnd, tile] = packed
        (rows0 if rnd == 0 else rows1).cur[0] = packed

    pl.semaphore_wait(barrier, len(peers))

    own = []
    rows0.start()
    for rnd in range(ROUNDS):
        own.append(
            spread(
                own_cur.at[rnd], own_got.at[rnd], own_gs.at[rnd], own_gr.at[rnd], tile, dom, n_tile
            )
        )
        (table0 if rnd == 0 else rows1).start()

    chunks = slots // CHUNK
    span = CHUNK * edges
    slot_row = lax.broadcasted_iota(jnp.int32, (LANES, span), 0)
    edge_slot = lax.broadcasted_iota(jnp.int32, (LANES, span), 1) // edges

    def fill(i, carry):
        group[i] = jnp.where(slot_row == edge_slot + i * CHUNK, 1.0, 0.0).astype(BF)
        return carry

    lax.fori_loop(0, senders * chunks, fill, 0)

    key = lax.broadcasted_iota(jnp.int32, (rows_all, edges), 0).astype(F32).astype(BF)
    mine = lax.broadcasted_iota(jnp.int32, (quarter, edges), 0) + tile * quarter
    mine = mine.astype(F32).astype(BF)
    one, zero = jnp.ones((), BF), jnp.zeros((), BF)

    def count(which, got, swap, first, last):
        if first == 0:
            acc[which] = jnp.zeros(acc.shape[1:], F32)

        def body(i, carry):
            s, chunk = lax.div(i, chunks), lax.rem(i, chunks)
            held = got[s, pl.ds(pl.multiple_of(chunk * PACK, PACK), PACK), :]
            keys, mines = [], []
            for g in range(CHUNK):
                src, dst = held[g : g + 1], held[CHUNK + g : CHUNK + g + 1]
                for_mine, for_key = (dst, src) if swap else (src, dst)
                keys.append(jnp.where(key == for_key, one, zero))
                mines.append(jnp.where(mine == for_mine, one, zero))
            pick_mine = jnp.concatenate(mines, axis=1)
            pick = jnp.concatenate([jnp.concatenate(keys, axis=1), pick_mine], axis=0)
            against = jnp.concatenate([group[i], pick_mine], axis=0)
            acc[which] += nt(pick, against)
            return carry

        lax.fori_loop(first * chunks, last * chunks, body, 0)

    def neg_row(got):
        last = slice(chunks * PACK, (chunks + 1) * PACK)
        total = got[0, last].astype(F32)
        for s in range(1, senders):
            total = total + got[s, last].astype(F32)
        return total[:1]

    key_block = (lax.broadcasted_iota(jnp.int32, (rows_all, LANES), 0) // edges).astype(F32)
    mine_block = (
        (lax.broadcasted_iota(jnp.int32, (quarter, LANES), 0) + tile * quarter) // edges
    ).astype(F32)

    def pair_counts(rnd, own_rows, other_rows):
        a, b = 2 * rnd, 2 * rnd + 1
        own_key = acc[a, :rows_all, :LANES] + jnp.where(key_block == neg_row(own_rows), 1.0, 0.0)
        own_mine = acc[a, rows_all:, :LANES]
        other_key = acc[b, :rows_all, :LANES]
        other_mine = acc[b, rows_all:, :LANES] + jnp.where(
            mine_block == neg_row(other_rows), 1.0, 0.0
        )
        every = nt(
            jnp.concatenate([own_key, other_key], axis=1).astype(BF),
            jnp.concatenate([own_mine, other_mine], axis=1).astype(BF),
        )
        positive = acc[a, :rows_all, LANES:] + acc[b, :rows_all, LANES:]
        return every - positive, positive

    eye = lax.broadcasted_iota(jnp.int32, (quarter, quarter), 0) == lax.broadcasted_iota(
        jnp.int32, (quarter, quarter), 1
    )

    def update(low, got, pairs, table, held):
        negative, positive = pairs
        other = jnp.concatenate([got[s] for s in range(n_tile)], axis=0)
        scores = nt(other, low)
        off_coef = (jax.nn.sigmoid(scores) / (2 * edges - 1)).astype(BF).astype(F32)
        on_coef = (-jax.nn.sigmoid(-scores)).astype(BF).astype(F32)
        weight = negative * off_coef + positive * on_coef
        high = weight.astype(BF)
        rest = (weight - high.astype(F32)).astype(BF)
        both = tn(jnp.concatenate([high, rest], axis=1), other)
        total = both[:quarter] + both[quarter:]
        held = held + jnp.sum(total * total, axis=1, keepdims=True) / width
        return table - LEARN_RATE * total / jnp.sqrt(held), held

    most = max(senders - 1, 1)
    for copy in own[0]:
        copy.wait_recv()
    count(0, own_got.at[0], False, 0, senders)
    while table0.at < table0.stages:
        rows0.advance()
        table0.advance()
    rows1.finish()
    for copy in own[1]:
        copy.wait_recv()
    count(2, own_got.at[1], False, 0, most)
    rows0.arrive()
    count(1, rows0.got, True, 0, senders)
    pairs = pair_counts(0, own_got.at[0], rows0.got)
    table0.arrive()
    held = jnp.sum(jnp.where(eye, state[...], 0.0), axis=1, keepdims=True)
    table, held = update(low, table0.got, pairs, emb[...], held)
    low = table.astype(BF)
    table1.cur[0] = low
    out[...] = table
    table1.start()
    count(2, own_got.at[1], False, most, senders)
    rows1.arrive()
    count(3, rows1.got, True, 0, most)
    table1.finish()
    count(3, rows1.got, True, most, senders)
    pairs = pair_counts(1, own_got.at[1], rows1.got)
    table1.arrive()
    table, held = update(table1.cur[0], table1.got, pairs, out[...], held)
    out[...] = table
    out_state[...] = jnp.sum(jnp.where(eye, held, 0.0), axis=0, keepdims=True)
    for copy in table0.sends + rows0.sends + rows1.sends + table1.sends + own[0] + own[1]:
        copy.wait_send()


def shards(n_dom, n_tile, embeddings, adagrad_state, offsets, lhs_rows, rhs_rows, neg_blocks, tile_counts):
    quarter, width = embeddings.shape
    slots, edges = lhs_rows.shape[2], lhs_rows.shape[3]
    rows_all = quarter * n_tile
    bits = n_dom.bit_length() - 1
    senders = (3 * n_tile + 3) // 4
    dma = pltpu.SemaphoreType.DMA

    def item(rows, lanes):
        return [
            pltpu.VMEM((bits + 1, rows, lanes), BF),
            pltpu.VMEM((bits, rows, lanes), BF),
            pltpu.VMEM((n_tile, rows, lanes), BF),
            dma((bits,)),
            dma((bits,)),
            dma((n_tile - 1,)),
            dma((n_tile - 1,)),
        ]

    message = (slots // CHUNK + 1) * PACK
    smem = pl.BlockSpec(memory_space=pltpu.SMEM)
    vmem = pl.BlockSpec(memory_space=pltpu.VMEM)

    def call(mask0, mask1, ident, *args):
        return pl.pallas_call(
            functools.partial(kernel, mask0, mask1, n_dom, n_tile, senders, edges),
            out_shape=(
                jax.ShapeDtypeStruct((quarter, width), F32),
                jax.ShapeDtypeStruct((1, quarter), F32),
            ),
            in_specs=[smem] * 3 + [vmem] * 4,
            out_specs=(vmem, vmem),
            scratch_shapes=item(quarter, width)
            + item(message, LANES)
            + item(message, LANES)
            + item(quarter, width)
            + [
                pltpu.VMEM((ROUNDS, n_tile, message, LANES), BF),
                dma((ROUNDS, n_tile - 1)),
                dma((ROUNDS, n_tile - 1)),
                pltpu.VMEM((senders * slots // CHUNK, LANES, CHUNK * edges), BF),
                pltpu.VMEM((2 * ROUNDS, rows_all + quarter, LANES + quarter), F32),
                pltpu.VMEM((ROUNDS, message, LANES), BF),
            ],
            compiler_params=pltpu.CompilerParams(
                collective_id=ident,
                has_side_effects=True,
                vmem_limit_bytes=40 << 20,
            ),
        )(*args)

    full = n_dom - 1
    if n_dom <= DIRECT_MAX:
        cases = [(full, mask) for mask in range(1, n_dom)]
        cases += [(mask, full) for mask in range(1, full)]
        case = jnp.where(offsets[0] == full, offsets[1] - 1, full + offsets[0] - 1)
    else:
        cases = [(full, None), (None, full)]
        case = jnp.where(offsets[0] == full, 0, 1)
    table, state = lax.switch(
        case,
        [functools.partial(call, *masks, ident) for ident, masks in enumerate(cases)],
        offsets,
        tile_counts[0],
        neg_blocks[0],
        embeddings,
        adagrad_state.reshape(1, quarter),
        lhs_rows[0],
        rhs_rows[0],
    )
    return table, state.reshape(quarter)


def solution(mesh):
    return jax.shard_map(
        functools.partial(shards, mesh.shape["dom"], mesh.shape["tile"]),
        mesh=mesh,
        in_specs=(
            P(("dom", "tile"), None),
            P(("dom", "tile")),
            P(),
            P("dom", None, "tile", None),
            P("dom", None, "tile", None),
            P("dom", None, "tile"),
            P("dom", None),
        ),
        out_specs=(P(("dom", "tile"), None), P(("dom", "tile"))),
        check_vma=False,
    )
```

```python
import functools

import jax
import jax.numpy as jnp
from jax import lax
from jax.experimental import pallas as pl
from jax.experimental.pallas import tpu as pltpu
from jax.sharding import PartitionSpec as P

ROUNDS = 2
LEARN_RATE = 0.5
MESH = pl.DeviceIdType.MESH
PACK = 16
LANES = 128
ALL_MAX = 8
CHUNK = 8
BF = jnp.bfloat16
F32 = jnp.float32


def nt(a, b):
    return lax.dot_general(a, b, (((1,), (1,)), ((), ())), preferred_element_type=F32)


def tn(a, b):
    return lax.dot_general(a, b, (((0,), (0,)), ((), ())), preferred_element_type=F32)


class Item:
    def __init__(self, refs, mask, offset, place):
        self.cur, self.recv, self.got, self.ssem, self.rsem, self.gs, self.gr = refs
        self.mask, self.offset = mask, offset
        self.fixed = mask is not None
        self.dom, self.tile, self.n_dom, self.n_tile = place
        self.to_all = not self.fixed and self.n_dom <= ALL_MAX
        self.stages = 1 if self.fixed or self.to_all else self.n_dom.bit_length() - 1
        self.at = 0
        self.sends = []

    def start_all(self):
        self.copies = []
        for mask in range(1, self.n_dom):
            copy = pltpu.make_async_remote_copy(
                src_ref=self.cur.at[0],
                dst_ref=self.recv.at[mask - 1],
                send_sem=self.ssem.at[mask - 1],
                recv_sem=self.rsem.at[mask - 1],
                device_id=(flip_bits(self.dom, mask), self.tile),
                device_id_type=MESH,
            )
            copy.start()
            self.copies.append(copy)
        self.sends += self.copies

    def start(self):
        if self.to_all:
            self.start_all()
            return
        if self.fixed:
            to = flip_bits(self.dom, self.mask)
        else:
            to = flip_bit(self.dom, self.at)
        self.copy = pltpu.make_async_remote_copy(
            src_ref=self.cur.at[self.at],
            dst_ref=self.recv.at[self.at],
            send_sem=self.ssem.at[self.at],
            recv_sem=self.rsem.at[self.at],
            device_id=(to, self.tile),
            device_id_type=MESH,
        )
        self.copy.start()
        self.sends.append(self.copy)

    def advance(self):
        for copy in self.copies if self.to_all else [self.copy]:
            copy.wait_recv()
        if self.fixed:
            final = self.recv.at[0]
        elif self.to_all:
            self.cur[1] = self.recv[jnp.maximum(self.offset - 1, 0)]
            final = self.cur.at[1]
        else:
            new = self.recv[self.at].astype(F32)
            old = self.cur[self.at].astype(F32)
            bit = (self.offset >> self.at) & 1
            take = jnp.broadcast_to(bit, new.shape) == 1
            self.cur[self.at + 1] = jnp.where(take, new, old).astype(BF)
            final = self.cur.at[self.at + 1]
        self.at += 1
        if self.at < self.stages:
            self.start()
            return
        self.copies = spread(final, self.got, self.gs, self.gr, self.tile, self.dom, self.n_tile)
        self.sends += self.copies
        self.got[self.tile] = final[...]

    def finish(self):
        while self.at < self.stages:
            self.advance()

    def arrive(self):
        for copy in self.copies:
            copy.wait_recv()


def flip_bit(value, bit):
    step = 1 << bit
    return value + step - 2 * step * lax.rem(lax.div(value, step), 2)


def flip_bits(value, mask):
    other = value
    for bit in range(mask.bit_length()):
        if mask >> bit & 1:
            other = flip_bit(other, bit)
    return other


def spread(src, got, send_sems, recv_sems, tile, dom, n_tile):
    copies = []
    for d in range(1, n_tile):
        copy = pltpu.make_async_remote_copy(
            src_ref=src,
            dst_ref=got.at[tile],
            send_sem=send_sems.at[d - 1],
            recv_sem=recv_sems.at[d - 1],
            device_id=(dom, lax.rem(tile + d, n_tile)),
            device_id_type=MESH,
        )
        copy.start()
        copies.append(copy)
    return copies


def kernel(mask0, mask1, n_dom, n_tile, senders, edges, *refs):
    offs, counts, neg, emb, state, lhs, rhs, out, out_state = refs[:9]
    items = [refs[9 + 7 * i : 16 + 7 * i] for i in range(4)]
    own_got, own_gs, own_gr, group, acc, own_cur = refs[37:]
    dom, tile = lax.axis_index("dom"), lax.axis_index("tile")
    quarter, width = emb.shape
    rows_all = quarter * n_tile
    slots = lhs.shape[1]
    bits = n_dom.bit_length() - 1

    barrier = pltpu.get_barrier_semaphore()
    peers = [(dom, lax.rem(tile + d, n_tile)) for d in range(1, n_tile)]
    if mask0 is None or mask1 is None:
        steps = range(1, n_dom) if n_dom <= ALL_MAX else [1 << bit for bit in range(bits)]
    else:
        steps = []
    steps = sorted(set(steps) | ({mask0, mask1} - {None}))
    peers += [(flip_bits(dom, mask), tile) for mask in steps]
    for peer in peers:
        pl.semaphore_signal(barrier, inc=1, device_id=peer, device_id_type=MESH)

    place = (dom, tile, n_dom, n_tile)
    table0 = Item(items[0], mask0, offs[0], place)
    rows0 = Item(items[1], mask0, offs[0], place)
    rows1 = Item(items[2], mask1, offs[1], place)
    table1 = Item(items[3], mask1, offs[1], place)

    lane = lax.broadcasted_iota(jnp.int32, (1, LANES), 1)
    slot_of = lax.broadcasted_iota(jnp.int32, (slots, edges), 0) + tile * slots
    low = emb[...].astype(BF)
    table0.cur[0] = low
    for rnd in range(ROUNDS):
        alive = slot_of < jnp.broadcast_to(counts[rnd], slot_of.shape)
        left = jnp.where(alive, lhs[rnd].astype(F32), -1.0)
        right = jnp.where(alive, rhs[rnd].astype(F32), -1.0)
        blocks = jnp.zeros((1, LANES), F32)
        for g in range(slots):
            value = jnp.broadcast_to(neg[rnd, g], blocks.shape).astype(F32)
            blocks = jnp.where(lane == tile * slots + g, value, blocks)
        parts = []
        for at in range(0, slots, CHUNK):
            parts += [left[at : at + CHUNK], right[at : at + CHUNK]]
        parts.append(jnp.broadcast_to(blocks, (PACK, LANES)))
        packed = jnp.concatenate(parts, axis=0).astype(BF)
        own_cur[rnd] = packed
        own_got[rnd, tile] = packed
        (rows0 if rnd == 0 else rows1).cur[0] = packed

    pl.semaphore_wait(barrier, len(peers))

    own = []
    rows0.start()
    for rnd in range(ROUNDS):
        own.append(
            spread(
                own_cur.at[rnd], own_got.at[rnd], own_gs.at[rnd], own_gr.at[rnd], tile, dom, n_tile
            )
        )
        (table0 if rnd == 0 else rows1).start()

    chunks = slots // CHUNK
    span = CHUNK * edges
    slot_row = lax.broadcasted_iota(jnp.int32, (LANES, span), 0)
    edge_slot = lax.broadcasted_iota(jnp.int32, (LANES, span), 1) // edges

    def fill(i, carry):
        group[i] = jnp.where(slot_row == edge_slot + i * CHUNK, 1.0, 0.0).astype(BF)
        return carry

    lax.fori_loop(0, senders * chunks, fill, 0)

    key = lax.broadcasted_iota(jnp.int32, (rows_all, edges), 0).astype(F32).astype(BF)
    mine = lax.broadcasted_iota(jnp.int32, (quarter, edges), 0) + tile * quarter
    mine = mine.astype(F32).astype(BF)
    one, zero = jnp.ones((), BF), jnp.zeros((), BF)

    def count(which, got, swap, first, last):
        if first == 0:
            acc[which] = jnp.zeros(acc.shape[1:], F32)

        def body(i, carry):
            s, chunk = lax.div(i, chunks), lax.rem(i, chunks)
            held = got[s, pl.ds(pl.multiple_of(chunk * PACK, PACK), PACK), :]
            keys, mines = [], []
            for g in range(CHUNK):
                src, dst = held[g : g + 1], held[CHUNK + g : CHUNK + g + 1]
                for_mine, for_key = (dst, src) if swap else (src, dst)
                keys.append(jnp.where(key == for_key, one, zero))
                mines.append(jnp.where(mine == for_mine, one, zero))
            pick_mine = jnp.concatenate(mines, axis=1)
            pick = jnp.concatenate([jnp.concatenate(keys, axis=1), pick_mine], axis=0)
            against = jnp.concatenate([group[i], pick_mine], axis=0)
            acc[which] += nt(pick, against)
            return carry

        lax.fori_loop(first * chunks, last * chunks, body, 0)

    def neg_row(got):
        last = slice(chunks * PACK, (chunks + 1) * PACK)
        total = got[0, last].astype(F32)
        for s in range(1, senders):
            total = total + got[s, last].astype(F32)
        return total[:1]

    key_block = (lax.broadcasted_iota(jnp.int32, (rows_all, LANES), 0) // edges).astype(F32)
    mine_block = (
        (lax.broadcasted_iota(jnp.int32, (quarter, LANES), 0) + tile * quarter) // edges
    ).astype(F32)

    def pair_counts(rnd, own_rows, other_rows):
        a, b = 2 * rnd, 2 * rnd + 1
        own_key = acc[a, :rows_all, :LANES] + jnp.where(key_block == neg_row(own_rows), 1.0, 0.0)
        own_mine = acc[a, rows_all:, :LANES]
        other_key = acc[b, :rows_all, :LANES]
        other_mine = acc[b, rows_all:, :LANES] + jnp.where(
            mine_block == neg_row(other_rows), 1.0, 0.0
        )
        every = nt(
            jnp.concatenate([own_key, other_key], axis=1).astype(BF),
            jnp.concatenate([own_mine, other_mine], axis=1).astype(BF),
        )
        positive = acc[a, :rows_all, LANES:] + acc[b, :rows_all, LANES:]
        return every - positive, positive

    eye = lax.broadcasted_iota(jnp.int32, (quarter, quarter), 0) == lax.broadcasted_iota(
        jnp.int32, (quarter, quarter), 1
    )

    def update(low, got, pairs, table, held):
        negative, positive = pairs
        other = jnp.concatenate([got[s] for s in range(n_tile)], axis=0)
        scores = nt(other, low)
        off_coef = (jax.nn.sigmoid(scores) / (2 * edges - 1)).astype(BF).astype(F32)
        on_coef = (-jax.nn.sigmoid(-scores)).astype(BF).astype(F32)
        weight = negative * off_coef + positive * on_coef
        high = weight.astype(BF)
        rest = (weight - high.astype(F32)).astype(BF)
        both = tn(jnp.concatenate([high, rest], axis=1), other)
        total = both[:quarter] + both[quarter:]
        held = held + jnp.sum(total * total, axis=1, keepdims=True) / width
        return table - LEARN_RATE * total / jnp.sqrt(held), held

    most = max(senders - 1, 1)
    for copy in own[0]:
        copy.wait_recv()
    count(0, own_got.at[0], False, 0, senders)
    while table0.at < table0.stages:
        rows0.advance()
        table0.advance()
    rows1.finish()
    for copy in own[1]:
        copy.wait_recv()
    count(2, own_got.at[1], False, 0, most)
    rows0.arrive()
    count(1, rows0.got, True, 0, senders)
    pairs = pair_counts(0, own_got.at[0], rows0.got)
    table0.arrive()
    held = jnp.sum(jnp.where(eye, state[...], 0.0), axis=1, keepdims=True)
    table, held = update(low, table0.got, pairs, emb[...], held)
    low = table.astype(BF)
    table1.cur[0] = low
    out[...] = table
    table1.start()
    count(2, own_got.at[1], False, most, senders)
    rows1.arrive()
    count(3, rows1.got, True, 0, most)
    table1.finish()
    count(3, rows1.got, True, most, senders)
    pairs = pair_counts(1, own_got.at[1], rows1.got)
    table1.arrive()
    table, held = update(table1.cur[0], table1.got, pairs, out[...], held)
    out[...] = table
    out_state[...] = jnp.sum(jnp.where(eye, held, 0.0), axis=0, keepdims=True)
    for copy in table0.sends + rows0.sends + rows1.sends + table1.sends + own[0] + own[1]:
        copy.wait_send()


def shards(n_dom, n_tile, embeddings, adagrad_state, offsets, lhs_rows, rhs_rows, neg_blocks, tile_counts):
    quarter, width = embeddings.shape
    slots, edges = lhs_rows.shape[2], lhs_rows.shape[3]
    rows_all = quarter * n_tile
    bits = n_dom.bit_length() - 1
    senders = (3 * n_tile + 3) // 4
    dma = pltpu.SemaphoreType.DMA
    arrivals = n_dom - 1 if n_dom <= ALL_MAX else bits

    def item(rows, lanes):
        return [
            pltpu.VMEM((bits + 1, rows, lanes), BF),
            pltpu.VMEM((arrivals, rows, lanes), BF),
            pltpu.VMEM((n_tile, rows, lanes), BF),
            dma((arrivals,)),
            dma((arrivals,)),
            dma((n_tile - 1,)),
            dma((n_tile - 1,)),
        ]

    message = (slots // CHUNK + 1) * PACK
    smem = pl.BlockSpec(memory_space=pltpu.SMEM)
    vmem = pl.BlockSpec(memory_space=pltpu.VMEM)

    def call(mask0, mask1, ident, *args):
        return pl.pallas_call(
            functools.partial(kernel, mask0, mask1, n_dom, n_tile, senders, edges),
            out_shape=(
                jax.ShapeDtypeStruct((quarter, width), F32),
                jax.ShapeDtypeStruct((1, quarter), F32),
            ),
            in_specs=[smem] * 3 + [vmem] * 4,
            out_specs=(vmem, vmem),
            scratch_shapes=item(quarter, width)
            + item(message, LANES)
            + item(message, LANES)
            + item(quarter, width)
            + [
                pltpu.VMEM((ROUNDS, n_tile, message, LANES), BF),
                dma((ROUNDS, n_tile - 1)),
                dma((ROUNDS, n_tile - 1)),
                pltpu.VMEM((senders * slots // CHUNK, LANES, CHUNK * edges), BF),
                pltpu.VMEM((2 * ROUNDS, rows_all + quarter, LANES + quarter), F32),
                pltpu.VMEM((ROUNDS, message, LANES), BF),
            ],
            compiler_params=pltpu.CompilerParams(
                collective_id=ident,
                has_side_effects=True,
                vmem_limit_bytes=40 << 20,
            ),
        )(*args)

    operands = (
        offsets,
        tile_counts[0],
        neg_blocks[0],
        embeddings,
        adagrad_state.reshape(1, quarter),
        lhs_rows[0],
        rhs_rows[0],
    )
    if n_dom <= ALL_MAX:
        table, state = call(None, None, 0, *operands)
    else:
        table, state = lax.cond(
            offsets[0] == n_dom - 1,
            functools.partial(call, n_dom - 1, None, 0),
            functools.partial(call, None, n_dom - 1, 1),
            *operands,
        )
    return table, state.reshape(quarter)


def solution(mesh):
    return jax.shard_map(
        functools.partial(shards, mesh.shape["dom"], mesh.shape["tile"]),
        mesh=mesh,
        in_specs=(
            P(("dom", "tile"), None),
            P(("dom", "tile")),
            P(),
            P("dom", None, "tile", None),
            P("dom", None, "tile", None),
            P("dom", None, "tile"),
            P("dom", None),
        ),
        out_specs=(P(("dom", "tile"), None), P(("dom", "tile"))),
        check_vma=False,
    )
```
